128 devices in a mesh: lag: 8 (over z_hi, y), patch: 16 (over z_lo, x, core).
Axes of the slice: x: 4, y: 4, z: 4 (z_hi: 2, z_lo: 2; z = z_hi * 2 + z_lo), core: 2. Of those that a mesh axis runs over, the one named last changes fastest.
Arguments:
- excitation: float32 [4, 16384, 128], P(None, 'patch'), may hold values from -6 to 6
- pending: float32 [24, 16384, 128], P('lag', 'patch'), may hold values from -6 to 6
- retarded_blocks: bfloat16 [24, 128, 16, 128, 128], P('lag', 'patch'), may hold values from -0.02734375 to 0.02734375
- column_index: int32 [24, 128, 16], P('lag', 'patch'), may hold values from 0 to 127, all different within a row
- near_inverse: float32 [64, 128, 128], P('patch'), may hold values from -1 to 4
- near_index: int32 [128], P('patch'), may hold values from 0 to 3
Outputs:
- currents: bfloat16 [4, 16384, 128], P(None, 'patch')
- final_sums: float32 [24, 16384, 128], P('lag', 'patch')
The draws below stay inside these ranges and needn't reach their ends.
Inputs may be any that keep to these rules, and one draw needn't show every extreme that they name: `column_index`: each block row of each lag names 16 different column blocks. `near_index`: an index into the 4 inverses of the block row's own slab.
All inputs are finite; a program needn't handle non-finite values.
Results may differ from the reference program's by a relative error of at most 0.0034.
Values may be sent and summed in bfloat16 or wider, within the bound.
A program may use at most 128 MiB of HBM per device.

```python
import math
import jax
import jax.numpy as jnp
from jax import lax

BLK = 128
KB = 16
E = 128
STEPS = 4
BR = 8
NINV_DEV = 4
NB = 128
N = 16384
L = 24
NINV = 64
N_PATCH = 16


def draw_near_inverse(key, part):
    first, second = jax.random.split(jax.random.fold_in(key, 7))
    diagonal = jax.random.uniform(first, (NINV, BLK), minval=0.5, maxval=1.5)
    spread = 0.4
    noise = jnp.clip(jax.random.normal(second, (NINV, BLK, BLK)), -6.0, 6.0) * (spread / math.sqrt(BLK))
    return (noise + diagonal[:, :, None] * jnp.eye(BLK, dtype=jnp.float32)[None]).astype(jnp.float32)


def plant(entries, key, smallest, largest):
    place = [jax.random.randint(jax.random.fold_in(key, axis), (), 0, length) for axis, length in enumerate(entries.shape)]
    main_axis = entries.shape.index(max(entries.shape))
    neighbour = place[:main_axis] + [(place[main_axis] + 1) % entries.shape[main_axis]] + place[main_axis + 1:]
    return entries.at[tuple(place)].set(smallest).at[tuple(neighbour)].set(largest)


def block_scale(own_key, shape, cuts, least, high):
    level, own = 1.0, jax.random.fold_in(own_key, 6)
    for position, blocks in cuts:
        draws = jnp.exp(jax.random.uniform(jax.random.fold_in(own, position), (blocks,), jnp.float32, least / len(cuts), high / len(cuts)))
        level = level * jnp.repeat(draws, shape[position] // blocks).reshape([-1 if axis == position else 1 for axis in range(len(shape))])
    return level


def picks_of(stream_key, rows, number_of, top, lift):
    sequence = jax.random.permutation(jax.random.fold_in(stream_key, 1), number_of)
    favour = sequence
    for power in range(3):
        favour = favour * favour // number_of
    favour = favour * lift // number_of
    tickets = jax.random.randint(jax.random.fold_in(stream_key, 2), (rows, number_of), 0, 4096) + favour
    sure = jax.random.permutation(jax.random.fold_in(stream_key, 3), rows)[jnp.arange(number_of) % rows]
    tickets = jnp.where(jnp.arange(rows)[:, None] == sure[None, :], 1 << 14, tickets)
    priority = tickets * number_of + jnp.arange(number_of)
    return lax.top_k(priority.astype(jnp.int32), top)[1].astype(jnp.int32)


def scatter_about(rng, extent, deviation, most, shards=(), kind=jnp.bfloat16):
    level = block_scale(rng, extent, shards, -0.22, 0.18) if shards else 1.0
    drawn = jax.random.normal(rng, extent, jnp.float32) * deviation * level
    return jnp.minimum(jnp.maximum(drawn, -most), most).astype(kind)


def setup_inputs(seed: int = 0) -> dict:
    arg_keys = jax.random.split(jax.random.key(seed), 7)
    excitation = scatter_about(arg_keys[0], (STEPS, N, E), 1.0, 6.0, ((1, 16),), jnp.float32)
    pending = scatter_about(arg_keys[1], (L, N, E), 1.0, 6.0, ((0, 8), (1, 16)), jnp.float32)
    retarded_blocks = scatter_about(arg_keys[2], (L, NB, KB, BLK, BLK), (L * KB * BLK) ** -0.5, 0.02734375, ((0, 8), (1, 16)))
    column_index = picks_of(arg_keys[3], L * NB, NB, KB, 0).reshape((L, NB, KB))
    near_inverse = draw_near_inverse(jax.random.fold_in(arg_keys[6], 71), 0)
    near_index = plant(jax.random.randint(arg_keys[5], (NB,), 0, NINV_DEV), jax.random.fold_in(arg_keys[5], 1), 0, NINV_DEV - 1).astype(jnp.int32)
    return {"excitation": excitation, "pending": pending, "retarded_blocks": retarded_blocks, "column_index": column_index, "near_inverse": near_inverse, "near_index": near_index}


def solve_blocks(rhs, inverses):
    blocks = rhs.reshape(-1, BLK, E)
    solved = jnp.einsum('bij,bje->bie', inverses, blocks, precision=lax.Precision.HIGHEST)
    return solved.reshape(-1, E).astype(jnp.bfloat16)


def reference(excitation, pending, retarded_blocks, column_index, near_inverse, near_index):
    slab_of = jnp.arange(BR * N_PATCH, dtype=jnp.int32) // BR
    inverses = near_inverse[(slab_of * NINV_DEV + near_index).astype(jnp.int32)]
    waiting = pending
    currents = []
    for moment in range(STEPS):
        current = solve_blocks(excitation[moment] - waiting[0], inverses)
        currents.append(current)
        blocks = current.reshape(-1, BLK, E)

        def lag_term(operands):
            weights, columns = operands
            picked = blocks[columns].astype(jnp.float32)
            product = jnp.einsum('bkij,bkje->bie', weights.astype(jnp.float32), picked, precision=lax.Precision.HIGHEST)
            return product.reshape(-1, E)

        lag_terms = lax.map(lag_term, (retarded_blocks, column_index))
        shifted = jnp.concatenate([waiting[1:], jnp.zeros_like(waiting[:1])], axis=0)
        waiting = lag_terms + shifted
    return jnp.stack(currents), waiting
```

```python
import functools

import jax
import jax.numpy as jnp
from jax import lax
from jax.experimental import pallas as pl
from jax.experimental.pallas import tpu as pltpu
from jax.sharding import PartitionSpec as P

MESH = pl.DeviceIdType.MESH
BLK = 128
WIDTH = 128
ROWS = 1024
BLOCKS = 8
A_BLOCKS = 5
SHIFTS = (1, 3, 2)

OWN, FROM_X, FROM_Z, DIAG_A, DIAG_B, SIB, BEHIND, N_RECV = 0, 1, 4, 5, 8, 11, 22, 23
LAG_SEND = 23
N_SEND = 26


def kernel(
    steps,
    column_ref, near_ref, excitation_hbm, pending_hbm, weights_hbm, inverse_hbm,
    currents_hbm, sums_hbm,
    x0, x1, x2, x3, weights, excitation, inverse, waiting, behind0, behind, ahead,
    load_sem, store_sem, send_sem, recv_sem,
):
    fields = (x0, x1, x2, x3)
    lag, patch = lax.axis_index("lag"), lax.axis_index("patch")
    z_hi, y = lag // 4, lag % 4
    z_lo, x, core = patch // 8, (patch // 2) % 4, patch % 2

    def at(x=x, z_lo=z_lo, core=core, y=y, z_hi=z_hi):
        return (z_hi * 4 + y, z_lo * 8 + x * 2 + core)

    def held(x=x, z_lo=z_lo, core=core):
        return ((z_lo + z_hi) % 2) * 8 + x * 2 + core

    other_z, other_core = 1 - z_lo, 1 - core
    x_to = [(x + s) % 4 for s in SHIFTS]
    x_from = [(x + 4 - s) % 4 for s in SHIFTS]

    loads = [
        pltpu.make_async_copy(pending_hbm, waiting, load_sem.at[0]),
        pltpu.make_async_copy(inverse_hbm, inverse, load_sem.at[1]),
        pltpu.make_async_copy(excitation_hbm, excitation, load_sem.at[2]),
        pltpu.make_async_copy(weights_hbm, weights, load_sem.at[3]),
    ]
    for copy in loads:
        copy.start()

    barrier = pltpu.get_barrier_semaphore()
    greeted = [at(x=to) for to in x_to] + [at(y=(y + s) % 4) for s in SHIFTS]
    greeted += [at(z_lo=other_z), at(core=other_core), at(z_lo=other_z, z_hi=1 - z_hi), at(y=3 - y, z_hi=1 - z_hi)]
    for device in greeted:
        pl.semaphore_signal(barrier, inc=1, device_id=device, device_id_type=MESH)
    pl.semaphore_wait(barrier, len(greeted))

    def piece(t, slab, low=0, high=BLOCKS):
        return fields[t].at[pl.ds(slab * BLOCKS + low, high - low)]

    def copy(t, ref, device, index, sender=None):
        return pltpu.make_async_remote_copy(
            src_ref=ref,
            dst_ref=ref,
            send_sem=send_sem.at[t, index if sender is None else sender],
            recv_sem=recv_sem.at[t, index],
            device_id=device,
            device_id_type=MESH,
        )

    me = at()

    def to_sibling(t, ref, index):
        copy(t, ref, at(core=other_core), SIB + index).start()

    def along_y(t):
        for i, s in enumerate(SHIFTS):
            copy(t, piece(t, held()), at(y=(y + s) % 4), OWN, LAG_SEND + i).start()

    def first_sends(t):
        own = piece(t, held())
        for i, to in enumerate(x_to):
            copy(t, own, at(x=to), FROM_X + i).start()
        copy(t, own, at(z_lo=other_z), FROM_Z).start()
        to_sibling(t, own, 0)

    def relays(t):
        def arrived(ref, index):
            copy(t, ref, me, index).wait_recv()

        def from_z():
            ref = piece(t, held(z_lo=other_z))
            arrived(ref, FROM_Z)
            for i, to in enumerate(x_to):
                copy(t, piece(t, held(z_lo=other_z), A_BLOCKS), at(x=to), DIAG_B + i).start()
            to_sibling(t, ref, 4)

        def from_x(i):
            ref = piece(t, held(x=x_from[i]))
            arrived(ref, FROM_X + i)
            copy(t, piece(t, held(x=x_from[i]), 0, A_BLOCKS), at(z_lo=other_z), DIAG_A + i).start()
            to_sibling(t, ref, 1 + i)

        from_z()
        for i in range(3):
            from_x(i)
        for i in range(3):
            slab = held(x=x_from[i], z_lo=other_z)
            for ref, index in ((piece(t, slab, 0, A_BLOCKS), 0), (piece(t, slab, A_BLOCKS), 3)):
                arrived(ref, DIAG_A + index + i)
                to_sibling(t, ref, 5 + index + i)
        arrived(piece(t, held(core=other_core)), SIB)
        arrived(piece(t, held(z_lo=other_z, core=other_core)), SIB + 4)
        for i in range(3):
            arrived(piece(t, held(x=x_from[i], core=other_core)), SIB + 1 + i)
            slab = held(x=x_from[i], z_lo=other_z, core=other_core)
            arrived(piece(t, slab, 0, A_BLOCKS), SIB + 5 + i)
            arrived(piece(t, slab, A_BLOCKS), SIB + 8 + i)

    def solve(t):
        for b in range(ROWS // BLK):
            rows = pl.ds(b * BLK, BLK)
            rhs = excitation[t, rows, :] - waiting[0, rows, :]
            solved = jnp.dot(
                inverse[near_ref[b]], rhs, precision=lax.Precision.HIGHEST, preferred_element_type=jnp.float32
            )
            fields[t][held() * BLOCKS + b] = solved.astype(jnp.bfloat16)

    def apply(t, lag_here):
        field = fields[t]

        def row(b, carry):
            rows = pl.ds(pl.multiple_of(b * BLK, BLK), BLK)
            base = (lag_here * 8 + b) * 16
            left = jnp.concatenate([weights[lag_here, b, k] for k in range(16)], axis=1)
            right = jnp.concatenate(
                [field[column_ref[base + k]] for k in range(16)], axis=0
            )
            term = jnp.dot(left, right, preferred_element_type=jnp.float32)
            if lag_here < 2:
                above = waiting[lag_here + 1, rows, :]
            elif t == 0:
                above = behind0[rows, :]
            else:
                above = behind[t - 1, rows, :].astype(jnp.float32)
            waiting[lag_here, rows, :] = term + above
            return carry

        lax.fori_loop(0, 8, row, 0, unroll=8)

    def behind_copy(t, device):
        if t == 0:
            return pltpu.make_async_remote_copy(
                src_ref=pending_hbm.at[0], dst_ref=behind0, send_sem=send_sem.at[t, BEHIND],
                recv_sem=recv_sem.at[t, BEHIND], device_id=device, device_id_type=MESH,
            )
        return pltpu.make_async_remote_copy(
            src_ref=ahead.at[t - 1], dst_ref=behind.at[t - 1], send_sem=send_sem.at[t, BEHIND],
            recv_sem=recv_sem.at[t, BEHIND], device_id=device, device_id_type=MESH,
        )

    def pass_down(t):
        @pl.when(lag > 0)
        def _():
            if t > 0:
                ahead[t - 1] = waiting[0].astype(jnp.bfloat16)
            behind_copy(t, (lag - 1, patch)).start()

    def later_lags(t):
        apply(t, 1)

        @pl.when(lag < 7)
        def _():
            behind_copy(t, me).wait_recv()

        apply(t, 2)

    @pl.when(lag == 7)
    def _():
        behind0[...] = jnp.zeros_like(behind0)
        behind[...] = jnp.zeros_like(behind)

    pass_down(0)
    for copy_in in loads[:3]:
        copy_in.wait()

    for t in range(steps):

        @pl.when(lag == 0)
        def _():
            solve(t)
            first_sends(t)
            along_y(t)
            copy(t, piece(t, held()), at(z_lo=other_z, z_hi=1 - z_hi), OWN).start()

        if t == 0:
            loads[3].wait()
        else:
            later_lags(t - 1)

        @pl.when(lag > 0)
        def _():
            copy(t, piece(t, held()), me, OWN).wait_recv()

            @pl.when(lag == 4)
            def _():
                along_y(t)

            first_sends(t)

        relays(t)
        pltpu.make_async_copy(piece(t, patch), currents_hbm.at[t], store_sem.at[t]).start()
        apply(t, 0)
        if t + 1 < steps:
            pass_down(t + 1)

    later_lags(steps - 1)
    out = pltpu.make_async_copy(waiting, sums_hbm, store_sem.at[steps])
    out.start()

    for t in range(steps):
        own = piece(t, held())
        whole = [FROM_X, FROM_X + 1, FROM_X + 2, FROM_Z] + [SIB + i for i in range(5)]
        for index in whole:
            copy(t, own, me, index).wait_send()
        for i in range(3):
            for index in (DIAG_A + i, SIB + 5 + i):
                copy(t, piece(t, held(), 0, A_BLOCKS), me, index).wait_send()
            for index in (DIAG_B + i, SIB + 8 + i):
                copy(t, piece(t, held(), A_BLOCKS), me, index).wait_send()

        @pl.when(lag == 0)
        def _():
            copy(t, own, me, OWN).wait_send()

        @pl.when(y == 0)
        def _():
            for i in range(3):
                copy(t, own, me, OWN, LAG_SEND + i).wait_send()

        @pl.when(lag > 0)
        def _():
            behind_copy(t, me).wait_send()

        pltpu.make_async_copy(piece(t, patch), currents_hbm.at[t], store_sem.at[t]).wait()
    out.wait()


def per_device(excitation, pending, retarded_blocks, column_index, near_inverse, near_index):
    steps = excitation.shape[0]
    smem, hbm = pl.BlockSpec(memory_space=pltpu.SMEM), pl.BlockSpec(memory_space=pltpu.HBM)
    field = pltpu.VMEM((16 * BLOCKS, BLK, WIDTH), jnp.bfloat16)
    currents, sums = pl.pallas_call(
        functools.partial(kernel, steps),
        out_shape=(
            jax.ShapeDtypeStruct((steps, BLOCKS, BLK, WIDTH), jnp.bfloat16),
            jax.ShapeDtypeStruct(pending.shape, jnp.float32),
        ),
        in_specs=[smem, smem, hbm, hbm, hbm, hbm],
        out_specs=(hbm, hbm),
        scratch_shapes=[
            field, field, field, field,
            pltpu.VMEM(retarded_blocks.shape, jnp.bfloat16),
            pltpu.VMEM(excitation.shape, jnp.float32),
            pltpu.VMEM(near_inverse.shape, jnp.float32),
            pltpu.VMEM(pending.shape, jnp.float32),
            pltpu.VMEM((ROWS, WIDTH), jnp.float32),
            pltpu.VMEM((steps - 1, ROWS, WIDTH), jnp.bfloat16),
            pltpu.VMEM((steps - 1, ROWS, WIDTH), jnp.bfloat16),
            pltpu.SemaphoreType.DMA((4,)),
            pltpu.SemaphoreType.DMA((steps + 1,)),
            pltpu.SemaphoreType.DMA((steps, N_SEND)),
            pltpu.SemaphoreType.DMA((steps, N_RECV)),
        ],
        compiler_params=pltpu.CompilerParams(
            collective_id=0, has_side_effects=True, vmem_limit_bytes=58 * 2**20
        ),
    )(column_index.reshape(-1), near_index, excitation, pending, retarded_blocks, near_inverse)
    return currents.reshape(excitation.shape), sums


def solution(mesh):
    placed = (
        P(None, "patch", None),
        P("lag", "patch", None),
        P("lag", "patch", None, None, None),
        P("lag", "patch", None),
        P("patch", None, None),
        P("patch"),
    )
    return jax.shard_map(
        per_device,
        mesh=mesh,
        in_specs=placed,
        out_specs=(P(None, "patch", None), P("lag", "patch", None)),
        check_vma=False,
    )
```

```python
import functools

import jax
import jax.numpy as jnp
from jax import lax
from jax.experimental import pallas as pl
from jax.experimental.pallas import tpu as pltpu
from jax.sharding import PartitionSpec as P

MESH = pl.DeviceIdType.MESH
BLK = 128
WIDTH = 128
HALF = 64
BLOCKS = 8
PAIRS = 4
ROWS = BLOCKS * BLK
KB = 16
A_PAIRS = (2, 2)
SHIFTS = (1, 3, 2)

OWN, X_A, X_B, Z_A, Z_B, DIAG_A, DIAG_B, SIB, N_RECV = 0, 1, 4, 7, 8, 9, 12, 15, 23
LAG_SEND = 23
N_SEND = 26


def kernel(
    steps,
    pair_ref, side_ref, near_ref, excitation_hbm, pending_hbm, weights_hbm, inverse_hbm,
    currents_hbm, sums_hbm,
    f0, f1, f2, f3, f4, f5, f6, f7, weights, excitation, inverse, waiting, behind0, behind, ahead, currents, sides,
    load_sem, store_sem, down_send, down_recv, send_sem, recv_sem,
):
    fields = (f0, f1, f2, f3, f4, f5, f6, f7)
    units = 2 * steps
    lag, patch = lax.axis_index("lag"), lax.axis_index("patch")
    z_hi, y = lag // 4, lag % 4
    z_lo, x, core = patch // 8, (patch // 2) % 4, patch % 2

    def at(x=x, z_lo=z_lo, core=core, y=y, z_hi=z_hi):
        return (z_hi * 4 + y, z_lo * 8 + x * 2 + core)

    def held(x=x, z_lo=z_lo, core=core):
        return ((z_lo + z_hi) % 2) * 8 + x * 2 + core

    me = at()
    other_z, other_core = 1 - z_lo, 1 - core
    x_to = [(x + s) % 4 for s in SHIFTS]
    x_from = [(x + 4 - s) % 4 for s in SHIFTS]
    left_half = lax.broadcasted_iota(jnp.int32, (BLK, WIDTH), 1) < HALF

    loads = [
        pltpu.make_async_copy(pending_hbm, waiting, load_sem.at[0]),
        pltpu.make_async_copy(inverse_hbm, inverse, load_sem.at[1]),
        pltpu.make_async_copy(excitation_hbm, excitation, load_sem.at[2]),
        pltpu.make_async_copy(weights_hbm, weights, load_sem.at[3]),
    ]
    for load in loads:
        load.start()

    barrier = pltpu.get_barrier_semaphore()
    greeted = [at(x=to) for to in x_to] + [at(y=(y + s) % 4) for s in SHIFTS]
    greeted += [at(z_lo=other_z), at(core=other_core), at(z_lo=other_z, z_hi=1 - z_hi), at(y=3 - y, z_hi=1 - z_hi)]
    for device in greeted:
        pl.semaphore_signal(barrier, inc=1, device_id=device, device_id_type=MESH)
    pl.semaphore_wait(barrier, len(greeted))

    def piece(u, slab, low=0, high=PAIRS):
        return fields[u].at[pl.ds(slab * PAIRS + low, high - low)]

    def copy(u, ref, device, index, sender=None):
        return pltpu.make_async_remote_copy(
            src_ref=ref,
            dst_ref=ref,
            send_sem=send_sem.at[u, index if sender is None else sender],
            recv_sem=recv_sem.at[u, index],
            device_id=device,
            device_id_type=MESH,
        )

    def arrived(u, ref, index):
        copy(u, ref, me, index).wait_recv()

    def to_sibling(u, ref, index):
        copy(u, ref, at(core=other_core), SIB + index).start()

    def along_y(u):
        for i, s in enumerate(SHIFTS):
            copy(u, piece(u, held()), at(y=(y + s) % 4), OWN, LAG_SEND + i).start()

    def first_sends(u):
        cut = A_PAIRS[u % 2]
        own, first, second = piece(u, held()), piece(u, held(), 0, cut), piece(u, held(), cut)
        copy(u, second, at(z_lo=other_z), Z_B).start()
        for i, to in enumerate(x_to):
            copy(u, first, at(x=to), X_A + i).start()
        copy(u, first, at(z_lo=other_z), Z_A).start()
        to_sibling(u, own, 0)

    def relays(u):
        cut = A_PAIRS[u % 2]
        slab = held(z_lo=other_z)
        arrived(u, piece(u, slab, cut), Z_B)
        for i, to in enumerate(x_to):
            copy(u, piece(u, slab, cut), at(x=to), DIAG_B + i).start()
        for i, to in enumerate(x_to):
            copy(u, piece(u, held(), cut), at(x=to), X_B + i).start()

    def relays_z(u):
        cut = A_PAIRS[u % 2]
        for i in range(3):
            slab = held(x=x_from[i])
            arrived(u, piece(u, slab, 0, cut), X_A + i)
            copy(u, piece(u, slab, 0, cut), at(z_lo=other_z), DIAG_A + i).start()

    def share(u):
        cut = A_PAIRS[u % 2]
        slab = held(z_lo=other_z)
        arrived(u, piece(u, slab, 0, cut), Z_A)
        to_sibling(u, piece(u, slab), 4)
        for i in range(3):
            slab = held(x=x_from[i])
            arrived(u, piece(u, slab, cut), X_B + i)
            to_sibling(u, piece(u, slab), 1 + i)
        for i in range(3):
            slab = held(x=x_from[i], z_lo=other_z)
            arrived(u, piece(u, slab, cut), DIAG_B + i)
            arrived(u, piece(u, slab, 0, cut), DIAG_A + i)
            to_sibling(u, piece(u, slab), 5 + i)

    def complete(u):
        arrived(u, piece(u, held(core=other_core)), SIB)
        arrived(u, piece(u, held(z_lo=other_z, core=other_core)), SIB + 4)
        for i in range(3):
            arrived(u, piece(u, held(x=x_from[i], core=other_core)), SIB + 1 + i)
            arrived(u, piece(u, held(x=x_from[i], z_lo=other_z, core=other_core)), SIB + 5 + i)

    def swap(a):
        return pltpu.roll(a, HALF, 1)

    def solve(u):
        t, half = u // 2, u % 2
        for i in range(PAIRS):
            solved = []
            for b in (i, i + PAIRS):
                rows = pl.ds(b * BLK, BLK)
                rhs = excitation[t, rows, :] - waiting[0, rows, :]
                solved.append(
                    jnp.dot(inverse[near_ref[b]], rhs, precision=lax.Precision.HIGHEST, preferred_element_type=jnp.float32)
                )
            low, high = solved
            packed = jnp.where(left_half, low, swap(high)) if half == 0 else jnp.where(left_half, swap(low), high)
            fields[u][held() * PAIRS + i] = packed.astype(jnp.bfloat16)

    def apply(u, lag_here):
        t, half = u // 2, u % 2
        field = fields[u]
        mine = left_half if half == 0 else jnp.logical_not(left_half)

        def row(b, carry):
            rows = pl.ds(pl.multiple_of(b * BLK, BLK), BLK)
            base = (lag_here * BLOCKS + b) * KB
            left = jnp.concatenate([weights[lag_here, b, k] for k in range(KB)], axis=1)
            picked = []
            for k in range(KB):
                side = sides[side_ref[base + k]]
                picked.append(field[pair_ref[base + k]] * jnp.concatenate([side] * (BLK // 16), axis=0))
            term = jnp.dot(left, jnp.concatenate(picked, axis=0), preferred_element_type=jnp.float32)
            term = term + swap(term)
            if lag_here < 2:
                term = term + waiting[lag_here + 1, rows, :]
            waiting[lag_here, rows, :] = jnp.where(mine, term, waiting[lag_here, rows, :])
            return carry

        lax.fori_loop(0, BLOCKS, row, 0, unroll=4)

    def down_copy(t, device):
        if t == 0:
            return pltpu.make_async_remote_copy(
                src_ref=pending_hbm.at[0], dst_ref=behind0, send_sem=down_send.at[t],
                recv_sem=down_recv.at[t], device_id=device, device_id_type=MESH,
            )
        return pltpu.make_async_remote_copy(
            src_ref=ahead.at[t - 1], dst_ref=behind.at[t - 1], send_sem=down_send.at[t],
            recv_sem=down_recv.at[t], device_id=device, device_id_type=MESH,
        )

    def pass_down(t):
        @pl.when(lag > 0)
        def _():
            if t > 0:
                ahead[t - 1] = waiting[0].astype(jnp.bfloat16)
            down_copy(t, (lag - 1, patch)).start()

    def store(t):
        for i in range(PAIRS):
            first = fields[2 * t][patch * PAIRS + i].astype(jnp.float32)
            second = fields[2 * t + 1][patch * PAIRS + i].astype(jnp.float32)
            currents[t, i] = jnp.where(left_half, first, swap(second)).astype(jnp.bfloat16)
            currents[t, i + PAIRS] = jnp.where(left_half, swap(first), second).astype(jnp.bfloat16)
        pltpu.make_async_copy(currents.at[t], currents_hbm.at[t], store_sem.at[t]).start()

    pass_down(0)
    in_left = lax.broadcasted_iota(jnp.int32, (16, WIDTH), 1) < HALF
    sides[0] = jnp.where(in_left, 1.0, 0.0).astype(jnp.bfloat16)
    sides[1] = jnp.where(in_left, 0.0, 1.0).astype(jnp.bfloat16)

    for load in loads[:3]:
        load.wait()

    for u in range(units + 1):
        if u < units:

            @pl.when(lag == 0)
            def _():
                solve(u)
                copy(u, piece(u, held()), at(z_lo=other_z, z_hi=1 - z_hi), OWN).start()
                first_sends(u)
                along_y(u)

            @pl.when(lag > 0)
            def _():
                arrived(u, piece(u, held()), OWN)

                @pl.when(lag == 4)
                def _():
                    along_y(u)

                first_sends(u)

        if u == 1:
            loads[3].wait()

        if u >= 2:
            apply(u - 2, 1)
            apply(u - 2, 2)
        if u == 3:

            @pl.when(lag < 7)
            def _():
                down_copy(0, me).wait_recv()
                waiting[2] = waiting[2] + behind0[...]

        if u < units:
            relays(u)
        if u >= 1:
            share(u - 1)
        if u < units:
            relays_z(u)
        if u >= 3 and u % 2 == 1:
            store((u - 3) // 2)
        if u >= 1:
            complete(u - 1)
            apply(u - 1, 0)
        if u >= 2 and u % 2 == 0 and u // 2 < steps:
            pass_down(u // 2)

    apply(units - 1, 1)
    apply(units - 1, 2)

    @pl.when(lag < 7)
    def _():
        for t in range(1, steps):
            down_copy(t, me).wait_recv()
            waiting[t - 1] = waiting[t - 1] + behind[t - 1].astype(jnp.float32)

    out = pltpu.make_async_copy(waiting, sums_hbm, store_sem.at[steps])
    out.start()
    store(steps - 1)

    for u in range(units):
        cut = A_PAIRS[u % 2]
        own = piece(u, held())
        for i in range(8):
            copy(u, own, me, SIB + i).wait_send()
        for index in [X_A, X_A + 1, X_A + 2, Z_A, DIAG_A, DIAG_A + 1, DIAG_A + 2]:
            copy(u, piece(u, held(), 0, cut), me, index).wait_send()
        for index in [X_B, X_B + 1, X_B + 2, Z_B, DIAG_B, DIAG_B + 1, DIAG_B + 2]:
            copy(u, piece(u, held(), cut), me, index).wait_send()

        @pl.when(lag == 0)
        def _():
            copy(u, own, me, OWN).wait_send()

        @pl.when(y == 0)
        def _():
            for i in range(3):
                copy(u, own, me, OWN, LAG_SEND + i).wait_send()

    for t in range(steps):

        @pl.when(lag > 0)
        def _():
            down_copy(t, me).wait_send()

        pltpu.make_async_copy(currents.at[t], currents_hbm.at[t], store_sem.at[t]).wait()
    out.wait()


def per_device(excitation, pending, retarded_blocks, column_index, near_inverse, near_index):
    steps = excitation.shape[0]
    columns = column_index.reshape(-1)
    pairs = columns // BLOCKS * PAIRS + columns % PAIRS
    sides = columns // PAIRS % 2
    smem, hbm = pl.BlockSpec(memory_space=pltpu.SMEM), pl.BlockSpec(memory_space=pltpu.HBM)
    field = pltpu.VMEM((16 * PAIRS, BLK, WIDTH), jnp.bfloat16)
    currents, sums = pl.pallas_call(
        functools.partial(kernel, steps),
        out_shape=(
            jax.ShapeDtypeStruct((steps, BLOCKS, BLK, WIDTH), jnp.bfloat16),
            jax.ShapeDtypeStruct(pending.shape, jnp.float32),
        ),
        in_specs=[smem, smem, smem, hbm, hbm, hbm, hbm],
        out_specs=(hbm, hbm),
        scratch_shapes=[
            *[field] * 8,
            pltpu.VMEM(retarded_blocks.shape, jnp.bfloat16),
            pltpu.VMEM(excitation.shape, jnp.float32),
            pltpu.VMEM(near_inverse.shape, jnp.float32),
            pltpu.VMEM(pending.shape, jnp.float32),
            pltpu.VMEM((ROWS, WIDTH), jnp.float32),
            pltpu.VMEM((steps - 1, ROWS, WIDTH), jnp.bfloat16),
            pltpu.VMEM((steps - 1, ROWS, WIDTH), jnp.bfloat16),
            pltpu.VMEM((steps, BLOCKS, BLK, WIDTH), jnp.bfloat16),
            pltpu.VMEM((2, 16, WIDTH), jnp.bfloat16),
            pltpu.SemaphoreType.DMA((4,)),
            pltpu.SemaphoreType.DMA((steps + 1,)),
            pltpu.SemaphoreType.DMA((steps,)),
            pltpu.SemaphoreType.DMA((steps,)),
            pltpu.SemaphoreType.DMA((2 * steps, N_SEND)),
            pltpu.SemaphoreType.DMA((2 * steps, N_RECV)),
        ],
        compiler_params=pltpu.CompilerParams(
            collective_id=0, has_side_effects=True, vmem_limit_bytes=58 * 2**20
        ),
    )(pairs, sides, near_index, excitation, pending, retarded_blocks, near_inverse)
    return currents.reshape(excitation.shape), sums


def solution(mesh):
    placed = (
        P(None, "patch", None),
        P("lag", "patch", None),
        P("lag", "patch", None, None, None),
        P("lag", "patch", None),
        P("patch", None, None),
        P("patch"),
    )
    return jax.shard_map(
        per_device,
        mesh=mesh,
        in_specs=placed,
        out_specs=(P(None, "patch", None), P("lag", "patch", None)),
        check_vma=False,
    )
```

```python
import functools

import jax
import jax.numpy as jnp
from jax import lax
from jax.experimental import pallas as pl
from jax.experimental.pallas import tpu as pltpu
from jax.sharding import PartitionSpec as P

MESH = pl.DeviceIdType.MESH
BLK = 128
WIDTH = 128
HALF = 64
BLOCKS = 8
PAIRS = 4
ROWS = BLOCKS * BLK
KB = 16
A_PAIRS = (2, 2)
SHIFTS = (1, 3, 2)

OWN, X_A, X_B, Z_A, Z_B, DIAG_A, DIAG_B, SIB, N_RECV = 0, 1, 4, 7, 8, 9, 12, 15, 23
LAG_SEND = 23
N_SEND = 26


def kernel(
    steps,
    pair_ref, side_ref, near_ref, excitation_hbm, pending_hbm, weights_hbm, inverse_hbm,
    currents_hbm, sums_hbm,
    f0, f1, f2, f3, f4, f5, f6, f7, weights, excitation, inverse, waiting, behind0, behind, ahead, crossing, currents, sides,
    load_sem, store_sem, down_send, down_recv, cross_send, cross_recv, send_sem, recv_sem,
):
    fields = (f0, f1, f2, f3, f4, f5, f6, f7)
    units = 2 * steps
    lag, patch = lax.axis_index("lag"), lax.axis_index("patch")
    z_hi, y = lag // 4, lag % 4
    z_lo, x, core = patch // 8, (patch // 2) % 4, patch % 2

    def at(x=x, z_lo=z_lo, core=core, y=y, z_hi=z_hi):
        return (z_hi * 4 + y, z_lo * 8 + x * 2 + core)

    def held(x=x, z_lo=z_lo, core=core):
        return ((z_lo + z_hi) % 2) * 8 + x * 2 + core

    me = at()
    other_z, other_core = 1 - z_lo, 1 - core
    x_to = [(x + s) % 4 for s in SHIFTS]
    x_from = [(x + 4 - s) % 4 for s in SHIFTS]
    left_half = lax.broadcasted_iota(jnp.int32, (BLK, WIDTH), 1) < HALF

    loads = [
        pltpu.make_async_copy(pending_hbm, waiting, load_sem.at[0]),
        pltpu.make_async_copy(inverse_hbm, inverse, load_sem.at[1]),
        pltpu.make_async_copy(excitation_hbm, excitation, load_sem.at[2]),
        pltpu.make_async_copy(weights_hbm, weights, load_sem.at[3]),
    ]
    for load in loads:
        load.start()

    barrier = pltpu.get_barrier_semaphore()
    greeted = [at(x=to) for to in x_to] + [at(y=(y + s) % 4) for s in SHIFTS]
    greeted += [at(z_lo=other_z), at(core=other_core), at(z_lo=other_z, z_hi=1 - z_hi), at(y=3 - y, z_hi=1 - z_hi)]
    greeted += [at(y=3 - y, z_hi=1 - z_hi, z_lo=other_z)]
    for device in greeted:
        pl.semaphore_signal(barrier, inc=1, device_id=device, device_id_type=MESH)
    pl.semaphore_wait(barrier, len(greeted))

    def piece(u, slab, low=0, high=PAIRS):
        return fields[u].at[pl.ds(slab * PAIRS + low, high - low)]

    def copy(u, ref, device, index, sender=None):
        return pltpu.make_async_remote_copy(
            src_ref=ref,
            dst_ref=ref,
            send_sem=send_sem.at[u, index if sender is None else sender],
            recv_sem=recv_sem.at[u, index],
            device_id=device,
            device_id_type=MESH,
        )

    def arrived(u, ref, index):
        copy(u, ref, me, index).wait_recv()

    def to_sibling(u, ref, index):
        copy(u, ref, at(core=other_core), SIB + index).start()

    def along_y(u):
        for i, s in enumerate(SHIFTS):
            copy(u, piece(u, held()), at(y=(y + s) % 4), OWN, LAG_SEND + i).start()

    def first_sends(u):
        cut = A_PAIRS[u % 2]
        own, first, second = piece(u, held()), piece(u, held(), 0, cut), piece(u, held(), cut)
        copy(u, second, at(z_lo=other_z), Z_B).start()
        for i, to in enumerate(x_to):
            copy(u, first, at(x=to), X_A + i).start()
        copy(u, first, at(z_lo=other_z), Z_A).start()
        to_sibling(u, own, 0)

    def relays(u):
        cut = A_PAIRS[u % 2]
        slab = held(z_lo=other_z)
        arrived(u, piece(u, slab, cut), Z_B)
        for i, to in enumerate(x_to):
            copy(u, piece(u, slab, cut), at(x=to), DIAG_B + i).start()
        for i, to in enumerate(x_to):
            copy(u, piece(u, held(), cut), at(x=to), X_B + i).start()

    def relays_z(u):
        cut = A_PAIRS[u % 2]
        for i in range(3):
            slab = held(x=x_from[i])
            arrived(u, piece(u, slab, 0, cut), X_A + i)
            copy(u, piece(u, slab, 0, cut), at(z_lo=other_z), DIAG_A + i).start()

    def share(u):
        cut = A_PAIRS[u % 2]
        slab = held(z_lo=other_z)
        arrived(u, piece(u, slab, 0, cut), Z_A)
        to_sibling(u, piece(u, slab), 4)
        for i in range(3):
            slab = held(x=x_from[i])
            arrived(u, piece(u, slab, cut), X_B + i)
            to_sibling(u, piece(u, slab), 1 + i)
        for i in range(3):
            slab = held(x=x_from[i], z_lo=other_z)
            arrived(u, piece(u, slab, cut), DIAG_B + i)
            arrived(u, piece(u, slab, 0, cut), DIAG_A + i)
            to_sibling(u, piece(u, slab), 5 + i)

    def complete(u):
        arrived(u, piece(u, held(core=other_core)), SIB)
        arrived(u, piece(u, held(z_lo=other_z, core=other_core)), SIB + 4)
        for i in range(3):
            arrived(u, piece(u, held(x=x_from[i], core=other_core)), SIB + 1 + i)
            arrived(u, piece(u, held(x=x_from[i], z_lo=other_z, core=other_core)), SIB + 5 + i)

    def swap(a):
        return pltpu.roll(a, HALF, 1)

    def solve(u):
        t, half = u // 2, u % 2
        for i in range(PAIRS):
            solved = []
            for b in (i, i + PAIRS):
                rows = pl.ds(b * BLK, BLK)
                rhs = excitation[t, rows, :] - waiting[0, rows, :]
                solved.append(
                    jnp.dot(inverse[near_ref[b]], rhs, precision=lax.Precision.HIGHEST, preferred_element_type=jnp.float32)
                )
            low, high = solved
            packed = jnp.where(left_half, low, swap(high)) if half == 0 else jnp.where(left_half, swap(low), high)
            fields[u][held() * PAIRS + i] = packed.astype(jnp.bfloat16)

    def apply(u, lag_here):
        t, half = u // 2, u % 2
        field = fields[u]
        mine = left_half if half == 0 else jnp.logical_not(left_half)

        def row(b, carry):
            rows = pl.ds(pl.multiple_of(b * BLK, BLK), BLK)
            base = (lag_here * BLOCKS + b) * KB
            left = jnp.concatenate([weights[lag_here, b, k] for k in range(KB)], axis=1)
            picked = []
            for k in range(KB):
                side = sides[side_ref[base + k]]
                picked.append(field[pair_ref[base + k]] * jnp.concatenate([side] * (BLK // 16), axis=0))
            term = jnp.dot(left, jnp.concatenate(picked, axis=0), preferred_element_type=jnp.float32)
            term = term + swap(term)
            if lag_here < 2:
                term = term + waiting[lag_here + 1, rows, :]
            waiting[lag_here, rows, :] = jnp.where(mine, term, waiting[lag_here, rows, :])
            return carry

        lax.fori_loop(0, BLOCKS, row, 0, unroll=4)

    def down_copy(t, device):
        if t == 0:
            return pltpu.make_async_remote_copy(
                src_ref=pending_hbm.at[0], dst_ref=behind0, send_sem=down_send.at[t],
                recv_sem=down_recv.at[t], device_id=device, device_id_type=MESH,
            )
        return pltpu.make_async_remote_copy(
            src_ref=ahead.at[t - 1], dst_ref=behind.at[t - 1], send_sem=down_send.at[t],
            recv_sem=down_recv.at[t], device_id=device, device_id_type=MESH,
        )

    def pass_down(t):
        @pl.when(lag > 0)
        def _():
            if t > 0:
                ahead[t - 1] = waiting[0].astype(jnp.bfloat16)

            @pl.when(jnp.logical_or(t == 0, lag != 4))
            def _():
                down_copy(t, (lag - 1, patch)).start()

            if t > 0:

                @pl.when(lag == 4)
                def _():
                    cross_copy(t, at(y=3, z_hi=0, z_lo=other_z)).start()

    def cross_copy(t, device):
        return pltpu.make_async_remote_copy(
            src_ref=ahead.at[t - 1], dst_ref=crossing.at[t - 1], send_sem=cross_send.at[t - 1],
            recv_sem=cross_recv.at[t - 1], device_id=device, device_id_type=MESH,
        )

    def crossed_copy(t, device):
        return pltpu.make_async_remote_copy(
            src_ref=crossing.at[t - 1], dst_ref=behind.at[t - 1], send_sem=cross_send.at[t - 1],
            recv_sem=down_recv.at[t], device_id=device, device_id_type=MESH,
        )

    def cross(t):
        @pl.when(lag == 3)
        def _():
            cross_copy(t, me).wait_recv()
            crossed_copy(t, at(z_lo=other_z)).start()

    def store(t):
        for i in range(PAIRS):
            first = fields[2 * t][patch * PAIRS + i].astype(jnp.float32)
            second = fields[2 * t + 1][patch * PAIRS + i].astype(jnp.float32)
            currents[t, i] = jnp.where(left_half, first, swap(second)).astype(jnp.bfloat16)
            currents[t, i + PAIRS] = jnp.where(left_half, swap(first), second).astype(jnp.bfloat16)
        pltpu.make_async_copy(currents.at[t], currents_hbm.at[t], store_sem.at[t]).start()

    pass_down(0)
    in_left = lax.broadcasted_iota(jnp.int32, (16, WIDTH), 1) < HALF
    sides[0] = jnp.where(in_left, 1.0, 0.0).astype(jnp.bfloat16)
    sides[1] = jnp.where(in_left, 0.0, 1.0).astype(jnp.bfloat16)

    for load in loads[:3]:
        load.wait()

    for u in range(units + 1):
        if u < units:

            @pl.when(lag == 0)
            def _():
                solve(u)
                copy(u, piece(u, held()), at(z_lo=other_z, z_hi=1 - z_hi), OWN).start()
                first_sends(u)
                along_y(u)

            @pl.when(lag > 0)
            def _():
                arrived(u, piece(u, held()), OWN)

                @pl.when(lag == 4)
                def _():
                    along_y(u)

                first_sends(u)

        if u == 1:
            loads[3].wait()

        if u >= 2:
            apply(u - 2, 1)
            apply(u - 2, 2)
        if u == 3:

            @pl.when(lag < 7)
            def _():
                down_copy(0, me).wait_recv()
                waiting[2] = waiting[2] + behind0[...]

        if u < units:
            relays(u)
        if u >= 1:
            share(u - 1)
        if u < units:
            relays_z(u)
        if u >= 3 and u % 2 == 1:
            cross(u // 2)
        if u >= 3 and u % 2 == 1:
            store((u - 3) // 2)
        if u >= 1:
            complete(u - 1)
            apply(u - 1, 0)
        if u >= 2 and u % 2 == 0 and u // 2 < steps:
            pass_down(u // 2)

    apply(units - 1, 1)
    apply(units - 1, 2)

    @pl.when(lag < 7)
    def _():
        for t in range(1, steps):
            down_copy(t, me).wait_recv()
            waiting[t - 1] = waiting[t - 1] + behind[t - 1].astype(jnp.float32)

    out = pltpu.make_async_copy(waiting, sums_hbm, store_sem.at[steps])
    out.start()
    store(steps - 1)

    for u in range(units):
        cut = A_PAIRS[u % 2]
        own = piece(u, held())
        for i in range(8):
            copy(u, own, me, SIB + i).wait_send()
        for index in [X_A, X_A + 1, X_A + 2, Z_A, DIAG_A, DIAG_A + 1, DIAG_A + 2]:
            copy(u, piece(u, held(), 0, cut), me, index).wait_send()
        for index in [X_B, X_B + 1, X_B + 2, Z_B, DIAG_B, DIAG_B + 1, DIAG_B + 2]:
            copy(u, piece(u, held(), cut), me, index).wait_send()

        @pl.when(lag == 0)
        def _():
            copy(u, own, me, OWN).wait_send()

        @pl.when(y == 0)
        def _():
            for i in range(3):
                copy(u, own, me, OWN, LAG_SEND + i).wait_send()

    for t in range(steps):

        @pl.when(jnp.logical_and(lag > 0, jnp.logical_or(t == 0, lag != 4)))
        def _():
            down_copy(t, me).wait_send()

        if t > 0:

            @pl.when(jnp.logical_or(lag == 3, lag == 4))
            def _():
                cross_copy(t, me).wait_send()

        pltpu.make_async_copy(currents.at[t], currents_hbm.at[t], store_sem.at[t]).wait()
    out.wait()


def per_device(excitation, pending, retarded_blocks, column_index, near_inverse, near_index):
    steps = excitation.shape[0]
    columns = column_index.reshape(-1)
    pairs = columns // BLOCKS * PAIRS + columns % PAIRS
    sides = columns // PAIRS % 2
    smem, hbm = pl.BlockSpec(memory_space=pltpu.SMEM), pl.BlockSpec(memory_space=pltpu.HBM)
    field = pltpu.VMEM((16 * PAIRS, BLK, WIDTH), jnp.bfloat16)
    currents, sums = pl.pallas_call(
        functools.partial(kernel, steps),
        out_shape=(
            jax.ShapeDtypeStruct((steps, BLOCKS, BLK, WIDTH), jnp.bfloat16),
            jax.ShapeDtypeStruct(pending.shape, jnp.float32),
        ),
        in_specs=[smem, smem, smem, hbm, hbm, hbm, hbm],
        out_specs=(hbm, hbm),
        scratch_shapes=[
            *[field] * 8,
            pltpu.VMEM(retarded_blocks.shape, jnp.bfloat16),
            pltpu.VMEM(excitation.shape, jnp.float32),
            pltpu.VMEM(near_inverse.shape, jnp.float32),
            pltpu.VMEM(pending.shape, jnp.float32),
            pltpu.VMEM((ROWS, WIDTH), jnp.float32),
            pltpu.VMEM((steps - 1, ROWS, WIDTH), jnp.bfloat16),
            pltpu.VMEM((steps - 1, ROWS, WIDTH), jnp.bfloat16),
            pltpu.VMEM((steps - 1, ROWS, WIDTH), jnp.bfloat16),
            pltpu.VMEM((steps, BLOCKS, BLK, WIDTH), jnp.bfloat16),
            pltpu.VMEM((2, 16, WIDTH), jnp.bfloat16),
            pltpu.SemaphoreType.DMA((4,)),
            pltpu.SemaphoreType.DMA((steps + 1,)),
            pltpu.SemaphoreType.DMA((steps,)),
            pltpu.SemaphoreType.DMA((steps,)),
            pltpu.SemaphoreType.DMA((steps - 1,)),
            pltpu.SemaphoreType.DMA((steps - 1,)),
            pltpu.SemaphoreType.DMA((2 * steps, N_SEND)),
            pltpu.SemaphoreType.DMA((2 * steps, N_RECV)),
        ],
        compiler_params=pltpu.CompilerParams(
            collective_id=0, has_side_effects=True, vmem_limit_bytes=58 * 2**20
        ),
    )(pairs, sides, near_index, excitation, pending, retarded_blocks, near_inverse)
    return currents.reshape(excitation.shape), sums


def solution(mesh):
    placed = (
        P(None, "patch", None),
        P("lag", "patch", None),
        P("lag", "patch", None, None, None),
        P("lag", "patch", None),
        P("patch", None, None),
        P("patch"),
    )
    return jax.shard_map(
        per_device,
        mesh=mesh,
        in_specs=placed,
        out_specs=(P(None, "patch", None), P("lag", "patch", None)),
        check_vma=False,
    )
```

```python
import functools

import jax
import jax.numpy as jnp
from jax import lax
from jax.experimental import pallas as pl
from jax.experimental.pallas import tpu as pltpu
from jax.sharding import PartitionSpec as P

MESH = pl.DeviceIdType.MESH
BLK = 128
WIDTH = 128
HALF = 64
BLOCKS = 8
PAIRS = 4
ROWS = BLOCKS * BLK
KB = 16
A_PAIRS = (2, 2)
SHIFTS = (1, 3, 2)

OWN, X_A, X_B, Z_A, Z_B, DIAG_A, DIAG_B, SIB, N_RECV = 0, 1, 4, 7, 8, 9, 12, 15, 23
LAG_SEND = 23
N_SEND = 26


def kernel(
    steps,
    pair_ref, side_ref, near_ref, excitation_hbm, pending_hbm, weights_hbm, inverse_hbm,
    currents_hbm, sums_hbm,
    f0, f1, f2, f3, f4, f5, f6, f7, weights, excitation, inverse, waiting, behind0, behind, ahead, crossing, currents, sides,
    load_sem, store_sem, down_send, down_recv, cross_send, cross_recv, send_sem, recv_sem,
):
    fields = (f0, f1, f2, f3, f4, f5, f6, f7)
    units = 2 * steps
    lag, patch = lax.axis_index("lag"), lax.axis_index("patch")
    z_hi, y = lag // 4, lag % 4
    z_lo, x, core = patch // 8, (patch // 2) % 4, patch % 2

    def at(x=x, z_lo=z_lo, core=core, y=y, z_hi=z_hi):
        return (z_hi * 4 + y, z_lo * 8 + x * 2 + core)

    def held(x=x, z_lo=z_lo, core=core):
        return ((z_lo + z_hi) % 2) * 8 + x * 2 + core

    me = at()
    other_z, other_core = 1 - z_lo, 1 - core
    x_to = [(x + s) % 4 for s in SHIFTS]
    x_from = [(x + 4 - s) % 4 for s in SHIFTS]
    left_half = lax.broadcasted_iota(jnp.int32, (BLK, WIDTH), 1) < HALF

    loads = [
        pltpu.make_async_copy(pending_hbm, waiting, load_sem.at[0]),
        pltpu.make_async_copy(inverse_hbm, inverse, load_sem.at[1]),
        pltpu.make_async_copy(excitation_hbm, excitation, load_sem.at[2]),
        pltpu.make_async_copy(weights_hbm, weights, load_sem.at[3]),
    ]
    for load in loads:
        load.start()

    barrier = pltpu.get_barrier_semaphore()
    greeted = [at(x=to) for to in x_to] + [at(y=(y + s) % 4) for s in SHIFTS]
    greeted += [at(z_lo=other_z), at(core=other_core), at(z_lo=other_z, z_hi=1 - z_hi), at(y=3 - y, z_hi=1 - z_hi)]
    greeted += [at(y=3 - y, z_hi=1 - z_hi, z_lo=other_z)]
    for device in greeted:
        pl.semaphore_signal(barrier, inc=1, device_id=device, device_id_type=MESH)
    pl.semaphore_wait(barrier, len(greeted))

    def piece(u, slab, low=0, high=PAIRS):
        return fields[u].at[pl.ds(slab * PAIRS + low, high - low)]

    def copy(u, ref, device, index, sender=None):
        return pltpu.make_async_remote_copy(
            src_ref=ref,
            dst_ref=ref,
            send_sem=send_sem.at[u, index if sender is None else sender],
            recv_sem=recv_sem.at[u, index],
            device_id=device,
            device_id_type=MESH,
        )

    def arrived(u, ref, index):
        copy(u, ref, me, index).wait_recv()

    def to_sibling(u, ref, index):
        copy(u, ref, at(core=other_core), SIB + index).start()

    def along_y(u):
        for i, s in enumerate(SHIFTS):
            copy(u, piece(u, held()), at(y=(y + s) % 4), OWN, LAG_SEND + i).start()

    def first_sends(u):
        cut = A_PAIRS[u % 2]
        own, first, second = piece(u, held()), piece(u, held(), 0, cut), piece(u, held(), cut)
        for i, to in enumerate(x_to):
            copy(u, first, at(x=to), X_A + i).start()
        copy(u, second, at(z_lo=other_z), Z_B).start()
        copy(u, first, at(z_lo=other_z), Z_A).start()
        to_sibling(u, own, 0)

    def relays(u):
        cut = A_PAIRS[u % 2]
        slab = held(z_lo=other_z)
        arrived(u, piece(u, slab, cut), Z_B)
        for i, to in enumerate(x_to):
            copy(u, piece(u, slab, cut), at(x=to), DIAG_B + i).start()
        for i, to in enumerate(x_to):
            copy(u, piece(u, held(), cut), at(x=to), X_B + i).start()

    def relays_z(u):
        cut = A_PAIRS[u % 2]
        for i in range(3):
            slab = held(x=x_from[i])
            arrived(u, piece(u, slab, 0, cut), X_A + i)
            copy(u, piece(u, slab, 0, cut), at(z_lo=other_z), DIAG_A + i).start()

    def share(u):
        cut = A_PAIRS[u % 2]
        slab = held(z_lo=other_z)
        arrived(u, piece(u, slab, 0, cut), Z_A)
        to_sibling(u, piece(u, slab), 4)
        for i in range(3):
            slab = held(x=x_from[i])
            arrived(u, piece(u, slab, cut), X_B + i)
            to_sibling(u, piece(u, slab), 1 + i)
        for i in range(3):
            slab = held(x=x_from[i], z_lo=other_z)
            arrived(u, piece(u, slab, cut), DIAG_B + i)
            arrived(u, piece(u, slab, 0, cut), DIAG_A + i)
            to_sibling(u, piece(u, slab), 5 + i)

    def complete(u):
        arrived(u, piece(u, held(core=other_core)), SIB)
        arrived(u, piece(u, held(z_lo=other_z, core=other_core)), SIB + 4)
        for i in range(3):
            arrived(u, piece(u, held(x=x_from[i], core=other_core)), SIB + 1 + i)
            arrived(u, piece(u, held(x=x_from[i], z_lo=other_z, core=other_core)), SIB + 5 + i)

    def swap(a):
        return pltpu.roll(a, HALF, 1)

    def solve(u):
        t, half = u // 2, u % 2
        for i in range(PAIRS):
            solved = []
            for b in (i, i + PAIRS):
                rows = pl.ds(b * BLK, BLK)
                rhs = excitation[t, rows, :] - waiting[0, rows, :]
                solved.append(
                    jnp.dot(inverse[near_ref[b]], rhs, precision=lax.Precision.HIGHEST, preferred_element_type=jnp.float32)
                )
            low, high = solved
            packed = jnp.where(left_half, low, swap(high)) if half == 0 else jnp.where(left_half, swap(low), high)
            fields[u][held() * PAIRS + i] = packed.astype(jnp.bfloat16)

    def apply(u, lag_here):
        t, half = u // 2, u % 2
        field = fields[u]
        mine = left_half if half == 0 else jnp.logical_not(left_half)

        def row(b, carry):
            rows = pl.ds(pl.multiple_of(b * BLK, BLK), BLK)
            base = (lag_here * BLOCKS + b) * KB
            left = jnp.concatenate([weights[lag_here, b, k] for k in range(KB)], axis=1)
            picked = []
            for k in range(KB):
                side = sides[side_ref[base + k]]
                picked.append(field[pair_ref[base + k]] * jnp.concatenate([side] * (BLK // 16), axis=0))
            term = jnp.dot(left, jnp.concatenate(picked, axis=0), preferred_element_type=jnp.float32)
            term = term + swap(term)
            if lag_here < 2:
                term = term + waiting[lag_here + 1, rows, :]
            waiting[lag_here, rows, :] = jnp.where(mine, term, waiting[lag_here, rows, :])
            return carry

        lax.fori_loop(0, BLOCKS, row, 0, unroll=4)

    def down_copy(t, device):
        if t == 0:
            return pltpu.make_async_remote_copy(
                src_ref=pending_hbm.at[0], dst_ref=behind0, send_sem=down_send.at[t],
                recv_sem=down_recv.at[t], device_id=device, device_id_type=MESH,
            )
        return pltpu.make_async_remote_copy(
            src_ref=ahead.at[t - 1], dst_ref=behind.at[t - 1], send_sem=down_send.at[t],
            recv_sem=down_recv.at[t], device_id=device, device_id_type=MESH,
        )

    def pass_down(t):
        @pl.when(lag > 0)
        def _():
            if t > 0:
                ahead[t - 1] = waiting[0].astype(jnp.bfloat16)

            @pl.when(jnp.logical_or(t == 0, lag != 4))
            def _():
                down_copy(t, (lag - 1, patch)).start()

            if t > 0:

                @pl.when(lag == 4)
                def _():
                    cross_copy(t, at(y=3, z_hi=0, z_lo=other_z)).start()

    def cross_copy(t, device):
        return pltpu.make_async_remote_copy(
            src_ref=ahead.at[t - 1], dst_ref=crossing.at[t - 1], send_sem=cross_send.at[t - 1],
            recv_sem=cross_recv.at[t - 1], device_id=device, device_id_type=MESH,
        )

    def crossed_copy(t, device):
        return pltpu.make_async_remote_copy(
            src_ref=crossing.at[t - 1], dst_ref=behind.at[t - 1], send_sem=cross_send.at[t - 1],
            recv_sem=down_recv.at[t], device_id=device, device_id_type=MESH,
        )

    def cross(t):
        @pl.when(lag == 3)
        def _():
            cross_copy(t, me).wait_recv()
            crossed_copy(t, at(z_lo=other_z)).start()

    def store(t):
        for i in range(PAIRS):
            first = fields[2 * t][patch * PAIRS + i].astype(jnp.float32)
            second = fields[2 * t + 1][patch * PAIRS + i].astype(jnp.float32)
            currents[t, i] = jnp.where(left_half, first, swap(second)).astype(jnp.bfloat16)
            currents[t, i + PAIRS] = jnp.where(left_half, swap(first), second).astype(jnp.bfloat16)
        pltpu.make_async_copy(currents.at[t], currents_hbm.at[t], store_sem.at[t]).start()

    pass_down(0)
    in_left = lax.broadcasted_iota(jnp.int32, (16, WIDTH), 1) < HALF
    sides[0] = jnp.where(in_left, 1.0, 0.0).astype(jnp.bfloat16)
    sides[1] = jnp.where(in_left, 0.0, 1.0).astype(jnp.bfloat16)

    for load in loads[:3]:
        load.wait()

    for u in range(units + 1):
        if u < units:

            @pl.when(lag == 0)
            def _():
                solve(u)
                copy(u, piece(u, held()), at(z_lo=other_z, z_hi=1 - z_hi), OWN).start()
                first_sends(u)
                along_y(u)

            @pl.when(lag > 0)
            def _():
                arrived(u, piece(u, held()), OWN)

                @pl.when(lag == 4)
                def _():
                    along_y(u)

                first_sends(u)

        if u == 1:
            loads[3].wait()

        if u >= 2:
            apply(u - 2, 1)
            apply(u - 2, 2)
        if u == 3:

            @pl.when(lag < 7)
            def _():
                down_copy(0, me).wait_recv()
                waiting[2] = waiting[2] + behind0[...]

        if u < units:
            relays(u)
        if u >= 1:
            share(u - 1)
        if u < units:
            relays_z(u)
        if u >= 3 and u % 2 == 1:
            cross(u // 2)
        if u >= 3 and u % 2 == 1:
            store((u - 3) // 2)
        if u >= 1:
            complete(u - 1)
            apply(u - 1, 0)
        if u >= 2 and u % 2 == 0 and u // 2 < steps:
            pass_down(u // 2)

    store(steps - 1)
    apply(units - 1, 1)
    apply(units - 1, 2)

    @pl.when(lag < 7)
    def _():
        for t in range(1, steps):
            down_copy(t, me).wait_recv()
            waiting[t - 1] = waiting[t - 1] + behind[t - 1].astype(jnp.float32)

    out = pltpu.make_async_copy(waiting, sums_hbm, store_sem.at[steps])
    out.start()

    for u in range(units):
        cut = A_PAIRS[u % 2]
        own = piece(u, held())
        for i in range(8):
            copy(u, own, me, SIB + i).wait_send()
        for index in [X_A, X_A + 1, X_A + 2, Z_A, DIAG_A, DIAG_A + 1, DIAG_A + 2]:
            copy(u, piece(u, held(), 0, cut), me, index).wait_send()
        for index in [X_B, X_B + 1, X_B + 2, Z_B, DIAG_B, DIAG_B + 1, DIAG_B + 2]:
            copy(u, piece(u, held(), cut), me, index).wait_send()

        @pl.when(lag == 0)
        def _():
            copy(u, own, me, OWN).wait_send()

        @pl.when(y == 0)
        def _():
            for i in range(3):
                copy(u, own, me, OWN, LAG_SEND + i).wait_send()

    for t in range(steps):

        @pl.when(jnp.logical_and(lag > 0, jnp.logical_or(t == 0, lag != 4)))
        def _():
            down_copy(t, me).wait_send()

        if t > 0:

            @pl.when(jnp.logical_or(lag == 3, lag == 4))
            def _():
                cross_copy(t, me).wait_send()

        pltpu.make_async_copy(currents.at[t], currents_hbm.at[t], store_sem.at[t]).wait()
    out.wait()


def per_device(excitation, pending, retarded_blocks, column_index, near_inverse, near_index):
    steps = excitation.shape[0]
    columns = column_index.reshape(-1)
    pairs = columns // BLOCKS * PAIRS + columns % PAIRS
    sides = columns // PAIRS % 2
    smem, hbm = pl.BlockSpec(memory_space=pltpu.SMEM), pl.BlockSpec(memory_space=pltpu.HBM)
    field = pltpu.VMEM((16 * PAIRS, BLK, WIDTH), jnp.bfloat16)
    currents, sums = pl.pallas_call(
        functools.partial(kernel, steps),
        out_shape=(
            jax.ShapeDtypeStruct((steps, BLOCKS, BLK, WIDTH), jnp.bfloat16),
            jax.ShapeDtypeStruct(pending.shape, jnp.float32),
        ),
        in_specs=[smem, smem, smem, hbm, hbm, hbm, hbm],
        out_specs=(hbm, hbm),
        scratch_shapes=[
            *[field] * 8,
            pltpu.VMEM(retarded_blocks.shape, jnp.bfloat16),
            pltpu.VMEM(excitation.shape, jnp.float32),
            pltpu.VMEM(near_inverse.shape, jnp.float32),
            pltpu.VMEM(pending.shape, jnp.float32),
            pltpu.VMEM((ROWS, WIDTH), jnp.float32),
            pltpu.VMEM((steps - 1, ROWS, WIDTH), jnp.bfloat16),
            pltpu.VMEM((steps - 1, ROWS, WIDTH), jnp.bfloat16),
            pltpu.VMEM((steps - 1, ROWS, WIDTH), jnp.bfloat16),
            pltpu.VMEM((steps, BLOCKS, BLK, WIDTH), jnp.bfloat16),
            pltpu.VMEM((2, 16, WIDTH), jnp.bfloat16),
            pltpu.SemaphoreType.DMA((4,)),
            pltpu.SemaphoreType.DMA((steps + 1,)),
            pltpu.SemaphoreType.DMA((steps,)),
            pltpu.SemaphoreType.DMA((steps,)),
            pltpu.SemaphoreType.DMA((steps - 1,)),
            pltpu.SemaphoreType.DMA((steps - 1,)),
            pltpu.SemaphoreType.DMA((2 * steps, N_SEND)),
            pltpu.SemaphoreType.DMA((2 * steps, N_RECV)),
        ],
        compiler_params=pltpu.CompilerParams(
            collective_id=0, has_side_effects=True, vmem_limit_bytes=58 * 2**20
        ),
    )(pairs, sides, near_index, excitation, pending, retarded_blocks, near_inverse)
    return currents.reshape(excitation.shape), sums


def solution(mesh):
    placed = (
        P(None, "patch", None),
        P("lag", "patch", None),
        P("lag", "patch", None, None, None),
        P("lag", "patch", None),
        P("patch", None, None),
        P("patch"),
    )
    return jax.shard_map(
        per_device,
        mesh=mesh,
        in_specs=placed,
        out_specs=(P(None, "patch", None), P("lag", "patch", None)),
        check_vma=False,
    )
```

```python
import functools

import jax
import jax.numpy as jnp
from jax import lax
from jax.experimental import pallas as pl
from jax.experimental.pallas import tpu as pltpu
from jax.sharding import PartitionSpec as P

MESH = pl.DeviceIdType.MESH
BLK = 128
WIDTH = 128
HALF = 64
BLOCKS = 8
PAIRS = 4
ROWS = BLOCKS * BLK
KB = 16
A_PAIRS = (2, 2)
SHIFTS = (1, 3, 2)

OWN, X_A, X_B, Z_A, Z_B, DIAG_A, DIAG_B, SIB, N_RECV = 0, 1, 4, 7, 8, 9, 12, 15, 23
LAG_SEND = 23
N_SEND = 26


def kernel(
    steps,
    pair_ref, side_ref, near_ref, excitation_hbm, pending_hbm, weights_hbm, inverse_hbm,
    currents_hbm, sums_hbm,
    f0, f1, f2, f3, f4, f5, f6, f7, weights, excitation, inverse, waiting, behind0, behind, ahead, crossing, currents, sides,
    load_sem, store_sem, down_send, down_recv, cross_send, cross_recv, send_sem, recv_sem,
):
    fields = (f0, f1, f2, f3, f4, f5, f6, f7)
    units = 2 * steps
    lag, patch = lax.axis_index("lag"), lax.axis_index("patch")
    z_hi, y = lag // 4, lag % 4
    z_lo, x, core = patch // 8, (patch // 2) % 4, patch % 2

    def at(x=x, z_lo=z_lo, core=core, y=y, z_hi=z_hi):
        return (z_hi * 4 + y, z_lo * 8 + x * 2 + core)

    def held(x=x, z_lo=z_lo, core=core):
        return ((z_lo + z_hi) % 2) * 8 + x * 2 + core

    me = at()
    other_z, other_core = 1 - z_lo, 1 - core
    x_to = [(x + s) % 4 for s in SHIFTS]
    x_from = [(x + 4 - s) % 4 for s in SHIFTS]
    left_half = lax.broadcasted_iota(jnp.int32, (BLK, WIDTH), 1) < HALF

    loads = [
        pltpu.make_async_copy(pending_hbm, waiting, load_sem.at[0]),
        pltpu.make_async_copy(inverse_hbm, inverse, load_sem.at[1]),
        pltpu.make_async_copy(excitation_hbm, excitation, load_sem.at[2]),
        pltpu.make_async_copy(weights_hbm, weights, load_sem.at[3]),
    ]
    for load in loads:
        load.start()

    barrier = pltpu.get_barrier_semaphore()
    greeted = [at(x=to) for to in x_to] + [at(y=(y + s) % 4) for s in SHIFTS]
    greeted += [at(z_lo=other_z), at(core=other_core), at(z_lo=other_z, z_hi=1 - z_hi), at(y=3 - y, z_hi=1 - z_hi)]
    greeted += [at(y=3 - y, z_hi=1 - z_hi, z_lo=other_z)]
    for device in greeted:
        pl.semaphore_signal(barrier, inc=1, device_id=device, device_id_type=MESH)
    pl.semaphore_wait(barrier, len(greeted))

    def piece(u, slab, low=0, high=PAIRS):
        return fields[u].at[pl.ds(slab * PAIRS + low, high - low)]

    def copy(u, ref, device, index, sender=None):
        return pltpu.make_async_remote_copy(
            src_ref=ref,
            dst_ref=ref,
            send_sem=send_sem.at[u, index if sender is None else sender],
            recv_sem=recv_sem.at[u, index],
            device_id=device,
            device_id_type=MESH,
        )

    def arrived(u, ref, index):
        copy(u, ref, me, index).wait_recv()

    def to_sibling(u, ref, index):
        copy(u, ref, at(core=other_core), SIB + index).start()

    def along_y(u):
        for i, s in enumerate(SHIFTS):
            copy(u, piece(u, held()), at(y=(y + s) % 4), OWN, LAG_SEND + i).start()

    def first_sends(u):
        cut = A_PAIRS[u % 2]
        own, first, second = piece(u, held()), piece(u, held(), 0, cut), piece(u, held(), cut)
        copy(u, second, at(z_lo=other_z), Z_B).start()
        for i, to in enumerate(x_to):
            copy(u, first, at(x=to), X_A + i).start()
        copy(u, first, at(z_lo=other_z), Z_A).start()
        to_sibling(u, own, 0)

    def relays(u):
        cut = A_PAIRS[u % 2]
        slab = held(z_lo=other_z)
        arrived(u, piece(u, slab, cut), Z_B)
        for i, to in enumerate(x_to):
            copy(u, piece(u, slab, cut), at(x=to), DIAG_B + i).start()
        for i, to in enumerate(x_to):
            copy(u, piece(u, held(), cut), at(x=to), X_B + i).start()

    def relays_z(u):
        cut = A_PAIRS[u % 2]
        for i in range(3):
            slab = held(x=x_from[i])
            arrived(u, piece(u, slab, 0, cut), X_A + i)
            copy(u, piece(u, slab, 0, cut), at(z_lo=other_z), DIAG_A + i).start()

    def share(u):
        cut = A_PAIRS[u % 2]
        slab = held(z_lo=other_z)
        arrived(u, piece(u, slab, 0, cut), Z_A)
        to_sibling(u, piece(u, slab), 4)
        for i in range(3):
            slab = held(x=x_from[i])
            arrived(u, piece(u, slab, cut), X_B + i)
            to_sibling(u, piece(u, slab), 1 + i)
        for i in range(3):
            slab = held(x=x_from[i], z_lo=other_z)
            arrived(u, piece(u, slab, cut), DIAG_B + i)
            arrived(u, piece(u, slab, 0, cut), DIAG_A + i)
            to_sibling(u, piece(u, slab), 5 + i)

    def complete(u):
        arrived(u, piece(u, held(core=other_core)), SIB)
        arrived(u, piece(u, held(z_lo=other_z, core=other_core)), SIB + 4)
        for i in range(3):
            arrived(u, piece(u, held(x=x_from[i], core=other_core)), SIB + 1 + i)
            arrived(u, piece(u, held(x=x_from[i], z_lo=other_z, core=other_core)), SIB + 5 + i)

    def swap(a):
        return pltpu.roll(a, HALF, 1)

    def solve(u):
        t, half = u // 2, u % 2
        for i in range(PAIRS):
            solved = []
            for b in (i, i + PAIRS):
                rows = pl.ds(b * BLK, BLK)
                rhs = excitation[t, rows, :] - waiting[0, rows, :]
                solved.append(
                    jnp.dot(inverse[near_ref[b]], rhs, precision=lax.Precision.HIGHEST, preferred_element_type=jnp.float32)
                )
            low, high = solved
            packed = jnp.where(left_half, low, swap(high)) if half == 0 else jnp.where(left_half, swap(low), high)
            fields[u][held() * PAIRS + i] = packed.astype(jnp.bfloat16)

    def apply(u, lag_here):
        t, half = u // 2, u % 2
        field = fields[u]
        mine = left_half if half == 0 else jnp.logical_not(left_half)

        def row(b, carry):
            rows = pl.ds(pl.multiple_of(b * BLK, BLK), BLK)
            base = (lag_here * BLOCKS + b) * KB
            left = jnp.concatenate([weights[lag_here, b, k] for k in range(KB)], axis=1)
            picked = []
            for k in range(KB):
                side = sides[side_ref[base + k]]
                picked.append(field[pair_ref[base + k]] * jnp.concatenate([side] * (BLK // 16), axis=0))
            term = jnp.dot(left, jnp.concatenate(picked, axis=0), preferred_element_type=jnp.float32)
            term = term + swap(term)
            if lag_here < 2:
                term = term + waiting[lag_here + 1, rows, :]
            waiting[lag_here, rows, :] = jnp.where(mine, term, waiting[lag_here, rows, :])
            return carry

        unroll = 8 if lag_here == 0 else 4 if u == units - 1 else 2
        lax.fori_loop(0, BLOCKS, row, 0, unroll=unroll)

    def down_copy(t, device):
        if t == 0:
            return pltpu.make_async_remote_copy(
                src_ref=pending_hbm.at[0], dst_ref=behind0, send_sem=down_send.at[t],
                recv_sem=down_recv.at[t], device_id=device, device_id_type=MESH,
            )
        return pltpu.make_async_remote_copy(
            src_ref=ahead.at[t - 1], dst_ref=behind.at[t - 1], send_sem=down_send.at[t],
            recv_sem=down_recv.at[t], device_id=device, device_id_type=MESH,
        )

    def pass_down(t):
        @pl.when(lag > 0)
        def _():
            if t > 0:
                ahead[t - 1] = waiting[0].astype(jnp.bfloat16)

            @pl.when(jnp.logical_or(t == 0, lag != 4))
            def _():
                down_copy(t, (lag - 1, patch)).start()

            if t > 0:

                @pl.when(lag == 4)
                def _():
                    cross_copy(t, at(y=3, z_hi=0, z_lo=other_z)).start()

    def cross_copy(t, device):
        return pltpu.make_async_remote_copy(
            src_ref=ahead.at[t - 1], dst_ref=crossing.at[t - 1], send_sem=cross_send.at[t - 1],
            recv_sem=cross_recv.at[t - 1], device_id=device, device_id_type=MESH,
        )

    def crossed_copy(t, device):
        return pltpu.make_async_remote_copy(
            src_ref=crossing.at[t - 1], dst_ref=behind.at[t - 1], send_sem=cross_send.at[t - 1],
            recv_sem=down_recv.at[t], device_id=device, device_id_type=MESH,
        )

    def cross(t):
        @pl.when(lag == 3)
        def _():
            cross_copy(t, me).wait_recv()
            crossed_copy(t, at(z_lo=other_z)).start()

    def store(t):
        for i in range(PAIRS):
            first = fields[2 * t][patch * PAIRS + i].astype(jnp.float32)
            second = fields[2 * t + 1][patch * PAIRS + i].astype(jnp.float32)
            currents[t, i] = jnp.where(left_half, first, swap(second)).astype(jnp.bfloat16)
            currents[t, i + PAIRS] = jnp.where(left_half, swap(first), second).astype(jnp.bfloat16)
        pltpu.make_async_copy(currents.at[t], currents_hbm.at[t], store_sem.at[t]).start()

    pass_down(0)
    in_left = lax.broadcasted_iota(jnp.int32, (16, WIDTH), 1) < HALF
    sides[0] = jnp.where(in_left, 1.0, 0.0).astype(jnp.bfloat16)
    sides[1] = jnp.where(in_left, 0.0, 1.0).astype(jnp.bfloat16)

    for load in loads[:3]:
        load.wait()

    for u in range(units + 1):
        if u < units:

            @pl.when(lag == 0)
            def _():
                solve(u)
                copy(u, piece(u, held()), at(z_lo=other_z, z_hi=1 - z_hi), OWN).start()
                first_sends(u)
                along_y(u)

            @pl.when(lag > 0)
            def _():
                arrived(u, piece(u, held()), OWN)

                @pl.when(lag == 4)
                def _():
                    along_y(u)

                first_sends(u)

        if u == 1:
            loads[3].wait()

        if u >= 2:
            apply(u - 2, 1)
            apply(u - 2, 2)
        if u == 3:

            @pl.when(lag < 7)
            def _():
                down_copy(0, me).wait_recv()
                waiting[2] = waiting[2] + behind0[...]

        if u < units:
            relays(u)
        if u >= 1:
            share(u - 1)
        if u < units:
            relays_z(u)
        if u >= 3 and u % 2 == 1:
            cross(u // 2)
        if u >= 3 and u % 2 == 1:
            store((u - 3) // 2)
        if u >= 1:
            complete(u - 1)
            apply(u - 1, 0)
        if u >= 2 and u % 2 == 0 and u // 2 < steps:
            pass_down(u // 2)

    apply(units - 1, 1)
    apply(units - 1, 2)

    @pl.when(lag < 7)
    def _():
        for t in range(1, steps):
            down_copy(t, me).wait_recv()
            waiting[t - 1] = waiting[t - 1] + behind[t - 1].astype(jnp.float32)

    out = pltpu.make_async_copy(waiting, sums_hbm, store_sem.at[steps])
    out.start()
    store(steps - 1)

    for u in range(units):
        cut = A_PAIRS[u % 2]
        own = piece(u, held())
        for i in range(8):
            copy(u, own, me, SIB + i).wait_send()
        for index in [X_A, X_A + 1, X_A + 2, Z_A, DIAG_A, DIAG_A + 1, DIAG_A + 2]:
            copy(u, piece(u, held(), 0, cut), me, index).wait_send()
        for index in [X_B, X_B + 1, X_B + 2, Z_B, DIAG_B, DIAG_B + 1, DIAG_B + 2]:
            copy(u, piece(u, held(), cut), me, index).wait_send()

        @pl.when(lag == 0)
        def _():
            copy(u, own, me, OWN).wait_send()

        @pl.when(y == 0)
        def _():
            for i in range(3):
                copy(u, own, me, OWN, LAG_SEND + i).wait_send()

    for t in range(steps):

        @pl.when(jnp.logical_and(lag > 0, jnp.logical_or(t == 0, lag != 4)))
        def _():
            down_copy(t, me).wait_send()

        if t > 0:

            @pl.when(jnp.logical_or(lag == 3, lag == 4))
            def _():
                cross_copy(t, me).wait_send()

        pltpu.make_async_copy(currents.at[t], currents_hbm.at[t], store_sem.at[t]).wait()
    out.wait()


def per_device(excitation, pending, retarded_blocks, column_index, near_inverse, near_index):
    steps = excitation.shape[0]
    columns = column_index.reshape(-1)
    pairs = columns // BLOCKS * PAIRS + columns % PAIRS
    sides = columns // PAIRS % 2
    smem, hbm = pl.BlockSpec(memory_space=pltpu.SMEM), pl.BlockSpec(memory_space=pltpu.HBM)
    field = pltpu.VMEM((16 * PAIRS, BLK, WIDTH), jnp.bfloat16)
    currents, sums = pl.pallas_call(
        functools.partial(kernel, steps),
        out_shape=(
            jax.ShapeDtypeStruct((steps, BLOCKS, BLK, WIDTH), jnp.bfloat16),
            jax.ShapeDtypeStruct(pending.shape, jnp.float32),
        ),
        in_specs=[smem, smem, smem, hbm, hbm, hbm, hbm],
        out_specs=(hbm, hbm),
        scratch_shapes=[
            *[field] * 8,
            pltpu.VMEM(retarded_blocks.shape, jnp.bfloat16),
            pltpu.VMEM(excitation.shape, jnp.float32),
            pltpu.VMEM(near_inverse.shape, jnp.float32),
            pltpu.VMEM(pending.shape, jnp.float32),
            pltpu.VMEM((ROWS, WIDTH), jnp.float32),
            pltpu.VMEM((steps - 1, ROWS, WIDTH), jnp.bfloat16),
            pltpu.VMEM((steps - 1, ROWS, WIDTH), jnp.bfloat16),
            pltpu.VMEM((steps - 1, ROWS, WIDTH), jnp.bfloat16),
            pltpu.VMEM((steps, BLOCKS, BLK, WIDTH), jnp.bfloat16),
            pltpu.VMEM((2, 16, WIDTH), jnp.bfloat16),
            pltpu.SemaphoreType.DMA((4,)),
            pltpu.SemaphoreType.DMA((steps + 1,)),
            pltpu.SemaphoreType.DMA((steps,)),
            pltpu.SemaphoreType.DMA((steps,)),
            pltpu.SemaphoreType.DMA((steps - 1,)),
            pltpu.SemaphoreType.DMA((steps - 1,)),
            pltpu.SemaphoreType.DMA((2 * steps, N_SEND)),
            pltpu.SemaphoreType.DMA((2 * steps, N_RECV)),
        ],
        compiler_params=pltpu.CompilerParams(
            collective_id=0, has_side_effects=True, vmem_limit_bytes=58 * 2**20
        ),
    )(pairs, sides, near_index, excitation, pending, retarded_blocks, near_inverse)
    return currents.reshape(excitation.shape), sums


def solution(mesh):
    placed = (
        P(None, "patch", None),
        P("lag", "patch", None),
        P("lag", "patch", None, None, None),
        P("lag", "patch", None),
        P("patch", None, None),
        P("patch"),
    )
    return jax.shard_map(
        per_device,
        mesh=mesh,
        in_specs=placed,
        out_specs=(P(None, "patch", None), P("lag", "patch", None)),
        check_vma=False,
    )
```
